32 devices in a mesh: rows: 8 (over z, x), cols: 4 (over y, core).
Axes of the slice: x: 2, y: 2, z: 4, core: 2. Of those that a mesh axis runs over, the one named last changes fastest.
Arguments:
- row_master: float32 [32, 1024, 256], P(None, ('rows', 'cols')), may hold values from -1.5 to 1.5
- row_accum: float32 [32, 1024, 256], P(None, ('rows', 'cols')), may hold values from 0.5 to 8
- col_master: float32 [32, 1024, 256], P(None, ('rows', 'cols')), may hold values from -1.5 to 1.5
- col_accum: float32 [32, 1024, 256], P(None, ('rows', 'cols')), may hold values from 0.5 to 8
- pairs: int32 [96, 2], P(('rows', 'cols')), may hold values from 0 to 31
- live: int32 [32], P(('rows', 'cols')), may hold values from 1 to 3, as said below
- counts: int32 [96, 1024, 1024], P(('rows', 'cols')), may hold values from 0 to 961
- row_marginal: int32 [32, 1024], replicated, may hold values from 1000 to 30000
- col_marginal: int32 [32, 1024], replicated, may hold values from 1000 to 30000
Outputs:
- row_new: float32 [32, 1024, 256], P(None, ('rows', 'cols'))
- row_accum_new: float32 [32, 1024, 256], P(None, ('rows', 'cols'))
- col_new: float32 [32, 1024, 256], P(None, ('rows', 'cols'))
- col_accum_new: float32 [32, 1024, 256], P(None, ('rows', 'cols'))
The draws below stay inside these ranges and needn't reach their ends.
Inputs may be any that keep to these rules, and one draw needn't show every extreme that they name: `live`: at least one device works on its whole list and at least one on a single pair.
All inputs are finite; a program needn't handle non-finite values.
Results may differ from the reference program's by a relative error of at most 0.0048.
Values may be sent and summed in bfloat16 or wider, within the bound.
No kernel may reach another device: no remote copies, remote signals or barrier semaphores. Data moves between devices by JAX's collectives and lax.ppermute only.
A program may use at most 128 MiB of HBM per device.

```python
import math
import jax
import jax.numpy as jnp
from jax import lax

D = 256
BLK = 1024
SLOTS = 3
NB = 32


def draw_live(key, part):
    key = jax.random.fold_in(key, 11)
    values = jax.random.randint(key, (NB,), 1, SLOTS + 1, dtype=jnp.int32)
    return values.at[0].set(SLOTS).at[1].set(1)


def draw_counts(key, part):
    key = jax.random.fold_in(key, 23)
    first_key, second_key, third_key = jax.random.split(key, 3)
    shape = (NB * SLOTS, BLK, BLK)
    first = jax.random.randint(first_key, shape, 0, 32, dtype=jnp.int32)
    second = jax.random.randint(second_key, shape, 0, 32, dtype=jnp.int32)
    empty = jax.random.randint(third_key, shape, 0, 10, dtype=jnp.int32)
    values = jnp.where(empty < 4, 0, first * second)
    return values.at[0, 0, 0].set(961).at[0, 0, 1].set(0)


def place_ends(result, key, low, top_value):
    longest = result.shape.index(max(result.shape))
    spots = []
    for shift in (0, 1):
        where = [jax.random.randint(jax.random.fold_in(key, axis), (), 0, length) for axis, length in enumerate(result.shape)]
        where[longest] = (where[longest] + shift) % result.shape[longest]
        spots.append(tuple(where))
    return result.at[spots[0]].set(low).at[spots[1]].set(top_value)


def level_of(own_key, extent, shards, least, largest):
    level, own = 1.0, jax.random.fold_in(own_key, 6)
    for position, shards_of in shards:
        steps = jnp.exp(jax.random.uniform(jax.random.fold_in(own, position), (shards_of,), jnp.float32, least / len(shards), largest / len(shards)))
        level = level * jnp.repeat(steps, extent[position] // shards_of).reshape([-1 if axis == position else 1 for axis in range(len(extent))])
    return level


def centred(own_key, shape, deviation, bound, cuts=(), kind=jnp.bfloat16):
    factor_of = level_of(own_key, shape, cuts, -0.22, 0.18) if cuts else 1.0
    drawn = jax.random.normal(own_key, shape, jnp.float32) * deviation * factor_of
    return jnp.minimum(jnp.maximum(drawn, -bound), bound).astype(kind)


def setup_inputs(seed: int = 0) -> dict:
    streams_of = jax.random.split(jax.random.key(seed), 10)
    return {
        "row_master": centred(streams_of[0], (NB, BLK, D), 0.25, 1.5, ((1, 32),), jnp.float32),
        "row_accum": jnp.clip(jnp.exp(math.log(8.0) - 2.7725887 * jax.random.uniform(streams_of[1], (NB, BLK, D), jnp.float32) ** level_of(streams_of[1], (NB, BLK, D), ((1, 32),), -0.2, 0.2)), 0.5, 8.0),
        "col_master": centred(streams_of[2], (NB, BLK, D), 0.25, 1.5, ((1, 32),), jnp.float32),
        "col_accum": jnp.clip(jnp.exp(math.log(8.0) - 2.7725887 * jax.random.uniform(streams_of[3], (NB, BLK, D), jnp.float32) ** level_of(streams_of[3], (NB, BLK, D), ((1, 32),), -0.2, 0.2)), 0.5, 8.0),
        "pairs": place_ends(jax.random.randint(streams_of[4], (NB * SLOTS, 2), 0, NB), jax.random.fold_in(streams_of[4], 1), 0, NB - 1).astype(jnp.int32),
        "live": draw_live(jax.random.fold_in(streams_of[9], 71), 0),
        "counts": draw_counts(jax.random.fold_in(streams_of[9], 71), 0),
        "row_marginal": place_ends(jax.random.randint(streams_of[7], (NB, BLK), 1000, 30001), jax.random.fold_in(streams_of[7], 1), 1000, 30000).astype(jnp.int32),
        "col_marginal": place_ends(jax.random.randint(streams_of[8], (NB, BLK), 1000, 30001), jax.random.fold_in(streams_of[8], 1), 1000, 30000).astype(jnp.int32),
    }


LOG_TOTAL = 14.3
LEARN_RATE = 0.05

def slot_delta(rows_blk, cols_blk, count, row_count, col_count):
    logits = lax.dot_general(rows_blk, cols_blk, (((1,), (1,)), ((), ())), preferred_element_type=jnp.float32)
    counts_f = count.astype(jnp.float32)
    target = jnp.log(jnp.maximum(counts_f, 1.0)) + LOG_TOTAL
    target = target - jnp.log(row_count.astype(jnp.float32))[:, None] - jnp.log(col_count.astype(jnp.float32))[None, :]
    spread = logits - target
    weight = 0.1 + 0.25 * jnp.sqrt(counts_f)
    grad = jnp.where(counts_f > 0.0, weight * spread, jax.nn.sigmoid(spread))
    return grad * (1.0 / jnp.sqrt(jnp.float32(count.shape[1])))

def adagrad(master, accum, grad):
    accum_new = accum + grad * grad
    return (master - LEARN_RATE * grad / jnp.sqrt(accum_new), accum_new)

def reference(row_master, row_accum, col_master, col_accum, pairs, live, counts, row_marginal, col_marginal):
    row_low = row_master.astype(jnp.bfloat16)
    col_low = col_master.astype(jnp.bfloat16)
    active = (jnp.arange(SLOTS, dtype=jnp.int32)[None, :] < live[:, None]).reshape(-1)

    def step(carry, item):
        row_grad, col_grad = carry
        pair, count, flag = item
        rows_blk = row_low[pair[0]]
        cols_blk = col_low[pair[1]]
        delta = slot_delta(rows_blk, cols_blk, count, row_marginal[pair[0]], col_marginal[pair[1]])
        delta = jnp.where(flag, delta, 0.0).astype(jnp.bfloat16)
        row_part = jnp.dot(delta, cols_blk, preferred_element_type=jnp.float32)
        col_part = lax.dot_general(delta, rows_blk, (((0,), (0,)), ((), ())), preferred_element_type=jnp.float32)
        row_grad = row_grad.at[pair[0]].add(row_part)
        col_grad = col_grad.at[pair[1]].add(col_part)
        return ((row_grad, col_grad), None)
    start = (jnp.zeros(row_master.shape, jnp.float32), jnp.zeros(col_master.shape, jnp.float32))
    (row_grad, col_grad), _ = lax.scan(step, start, (pairs, counts, active))
    row_new, row_accum_new = adagrad(row_master, row_accum, row_grad)
    col_new, col_accum_new = adagrad(col_master, col_accum, col_grad)
    return (row_new, row_accum_new, col_new, col_accum_new)
```

```python
import functools

import jax
import jax.numpy as jnp
from jax import lax
from jax.experimental import pallas as pl
from jax.experimental.pallas import tpu as pltpu
from jax.sharding import PartitionSpec as P

LOG_TOTAL = 14.3
LEARN_RATE = 0.05
AXES = ("rows", "cols")
TILE = 256
VMEM_LIMIT = 48 * 1024 * 1024

BF16 = jnp.bfloat16
F32 = jnp.float32


def vmem_spec():
    return pl.BlockSpec(memory_space=pltpu.VMEM)


def params():
    return pltpu.CompilerParams(vmem_limit_bytes=VMEM_LIMIT)


def pick_kernel(first, count, req, row_ref, col_ref, out_ref):
    nodes = out_ref.shape[0]

    def one(node, carry):
        for k in range(count):
            a = req[node, 2 * (first + k)]
            b = req[node, 2 * (first + k) + 1]
            out_ref[node, 2 * k] = row_ref[a].astype(BF16)
            out_ref[node, 2 * k + 1] = col_ref[b].astype(BF16)
        return carry

    lax.fori_loop(0, nodes, one, 0)


def pick(req, row_master, col_master, first, count):
    nodes = req.shape[0]
    piece, width = row_master.shape[1:]
    out = jax.ShapeDtypeStruct((nodes, 2 * count, piece, width), BF16)
    return pl.pallas_call(
        functools.partial(pick_kernel, first, count),
        out_shape=out,
        grid_spec=pltpu.PrefetchScalarGridSpec(
            num_scalar_prefetch=1,
            in_specs=[vmem_spec(), vmem_spec()],
            out_specs=vmem_spec(),
            grid=(),
        ),
        compiler_params=params(),
        cost_estimate=pl.CostEstimate(
            flops=0,
            bytes_accessed=2 * row_master.size * 4 + nodes * 2 * count * piece * width * 2,
            transcendentals=0,
        ),
        name="pick",
    )(req, row_master, col_master)


def item_kernel(
    first, pairs, live, got_ref, counts_ref, rm_ref, cm_ref, out_ref, rows_s, cols_s, acc_s
):
    slot = pl.program_id(0)
    step = pl.program_id(1)
    steps = pl.num_programs(1)
    groups, _, piece, width = got_ref.shape
    per_step = TILE // piece if piece <= TILE else 1

    @pl.when(step == 0)
    def _():
        rows_s[...] = got_ref[:, 0].reshape(groups * piece, width)
        cols_s[...] = got_ref[:, 1].reshape(groups * piece, width)

    alive = first + slot < live[0]

    @pl.when(alive)
    def _():
        a = pairs[first + slot, 0]
        b = pairs[first + slot, 1]
        start = pl.multiple_of(step * TILE, TILE)
        rows = rows_s[pl.ds(start, TILE), :]
        cols = cols_s[...]
        logits = lax.dot_general(rows, cols, (((1,), (1,)), ((), ())), preferred_element_type=F32)
        row_log = jnp.log(rm_ref[pl.ds(a, 1), pl.ds(start, TILE)].astype(F32)) - LOG_TOTAL
        col_log = jnp.log(cm_ref[pl.ds(b, 1), :].astype(F32))
        row_log = jnp.transpose(jnp.broadcast_to(row_log, (8, TILE)))[:, :1]
        counts = counts_ref[0].astype(F32)
        spread = (logits + row_log + col_log) - jnp.log(jnp.maximum(counts, 1.0))
        scale = 1.0 / (counts.shape[1] ** 0.5)
        weight = 0.1 * scale + (0.25 * scale) * jnp.sqrt(counts)
        grad = jnp.where(counts > 0.0, weight * spread, scale * jax.nn.sigmoid(spread))
        delta = grad.astype(BF16)
        row_part = jnp.dot(delta, cols, preferred_element_type=F32).astype(BF16)
        for g in range(per_step):
            out_ref[step * per_step + g, 0] = row_part[g * piece : (g + 1) * piece, :]
        part = lax.dot_general(rows, delta, (((0,), (0,)), ((), ())), preferred_element_type=F32)

        @pl.when(step == 0)
        def _():
            acc_s[...] = part

        @pl.when(step > 0)
        def _():
            acc_s[...] += part

        @pl.when(step == steps - 1)
        def _():
            out_ref[:, 1] = jnp.transpose(acc_s[...]).astype(BF16).reshape(groups, piece, width)

    @pl.when(jnp.logical_not(alive) & (step == 0))
    def _():
        out_ref[...] = jnp.zeros_like(out_ref)


def items(pairs, live, got, counts, row_marginal, col_marginal, first, count):
    nodes, _, piece, width = got.shape
    blk = counts.shape[1]
    fold = piece % 16 != 0
    if fold:
        got = got.transpose(1, 0, 2, 3).reshape(1, 2 * count, nodes * piece, width)
    groups, _, rows_in, _ = got.shape
    if rows_in > TILE:
        got = got.reshape(1, 2 * count, rows_in // TILE, TILE, width)[0].transpose(1, 0, 2, 3)
        groups, rows_in = got.shape[0], TILE
    out = pl.pallas_call(
        functools.partial(item_kernel, first),
        out_shape=jax.ShapeDtypeStruct(got.shape, BF16),
        grid_spec=pltpu.PrefetchScalarGridSpec(
            num_scalar_prefetch=2,
            grid=(count, blk // TILE),
            in_specs=[
                pl.BlockSpec((groups, 2, rows_in, width), lambda s, i, *_: (0, s, 0, 0)),
                pl.BlockSpec((1, TILE, blk), lambda s, i, *_: (first + s, i, 0)),
                pl.BlockSpec(row_marginal.shape, lambda s, i, *_: (0, 0)),
                pl.BlockSpec(col_marginal.shape, lambda s, i, *_: (0, 0)),
            ],
            out_specs=pl.BlockSpec((groups, 2, rows_in, width), lambda s, i, *_: (0, s, 0, 0)),
            scratch_shapes=[
                pltpu.VMEM((blk, width), BF16),
                pltpu.VMEM((blk, width), BF16),
                pltpu.VMEM((width, blk), F32),
            ],
        ),
        compiler_params=params(),
        cost_estimate=pl.CostEstimate(
            flops=6 * count * blk * blk * width,
            bytes_accessed=count * (blk * blk * 4 + 4 * blk * width * 2),
            transcendentals=4 * count * blk * blk,
        ),
        name="items",
    )(pairs, live, got, counts, row_marginal, col_marginal)
    if fold:
        out = out.transpose(1, 0, 2, 3).reshape(2 * count, nodes, piece, width)
        out = out.transpose(1, 0, 2, 3)
    return out


def sum_kernel(first, count, req, ret_ref, row_out, col_out):
    row_out[...] = jnp.zeros_like(row_out)
    col_out[...] = jnp.zeros_like(col_out)
    add_parts(first, count, req, ret_ref, row_out, col_out)


def add_parts(first, count, req, ret_ref, row_acc, col_acc):
    def one(node, carry):
        for k in range(count):
            a = req[node, 2 * (first + k)]
            b = req[node, 2 * (first + k) + 1]
            row_acc[a] += ret_ref[node, 2 * k].astype(F32)
            col_acc[b] += ret_ref[node, 2 * k + 1].astype(F32)
        return carry

    lax.fori_loop(0, ret_ref.shape[0], one, 0)


def sums(req, ret, blocks, first, count):
    piece, width = ret.shape[2:]
    shape = jax.ShapeDtypeStruct((blocks, piece, width), F32)
    return pl.pallas_call(
        functools.partial(sum_kernel, first, count),
        out_shape=(shape, shape),
        grid_spec=pltpu.PrefetchScalarGridSpec(
            num_scalar_prefetch=1,
            in_specs=[vmem_spec()],
            out_specs=(vmem_spec(), vmem_spec()),
            grid=(),
        ),
        compiler_params=params(),
        cost_estimate=pl.CostEstimate(
            flops=ret.size,
            bytes_accessed=ret.size * 2 + 8 * blocks * piece * width,
            transcendentals=0,
        ),
        name="sums",
    )(req, ret)


def update_kernel(first, count, req, ret_ref, rg, cg, rm, ra, cm, ca, rn, ran, cn, can):
    rn[...] = rg[...]
    cn[...] = cg[...]
    add_parts(first, count, req, ret_ref, rn, cn)

    def one(block, carry):
        for master, accum, new, accum_out in ((rm, ra, rn, ran), (cm, ca, cn, can)):
            grad = new[block]
            accum_new = accum[block] + grad * grad
            accum_out[block] = accum_new
            new[block] = master[block] - LEARN_RATE * grad / jnp.sqrt(accum_new)
        return carry

    lax.fori_loop(0, rm.shape[0], one, 0)


def update(req, ret, row_grad, col_grad, row_master, row_accum, col_master, col_accum, first, count):
    shape = jax.ShapeDtypeStruct(row_master.shape, F32)
    return pl.pallas_call(
        functools.partial(update_kernel, first, count),
        out_shape=(shape,) * 4,
        grid_spec=pltpu.PrefetchScalarGridSpec(
            num_scalar_prefetch=1,
            in_specs=[vmem_spec()] * 7,
            out_specs=(vmem_spec(),) * 4,
            grid=(),
        ),
        compiler_params=params(),
        cost_estimate=pl.CostEstimate(
            flops=8 * row_master.size,
            bytes_accessed=ret.size * 2 + 40 * row_master.size,
            transcendentals=2 * row_master.size,
        ),
        name="update",
    )(req, ret, row_grad, col_grad, row_master, row_accum, col_master, col_accum)


def exchange(x):
    return lax.all_to_all(x, AXES, split_axis=0, concat_axis=0, tiled=True)


def body(
    row_master, row_accum, col_master, col_accum, pairs, live, counts, row_marginal, col_marginal
):
    slots = pairs.shape[0]
    blocks = row_master.shape[0]
    nodes = lax.axis_size(AXES)
    req = exchange(jnp.broadcast_to(pairs.reshape(1, 2 * slots), (nodes, 2 * slots)))
    cut = 1
    lists = ((0, cut), (cut, slots - cut))
    back = []
    got = [exchange(pick(req, row_master, col_master, *part)) for part in lists]
    for part, rows in zip(lists, got):
        back.append(exchange(items(pairs, live, rows, counts, row_marginal, col_marginal, *part)))
    row_grad, col_grad = sums(req, back[0], blocks, *lists[0])
    return update(
        req, back[1], row_grad, col_grad, row_master, row_accum, col_master, col_accum, *lists[1]
    )


def solution(mesh):
    table = P(None, AXES, None)
    return jax.shard_map(
        body,
        mesh=mesh,
        in_specs=(
            table,
            table,
            table,
            table,
            P(AXES, None),
            P(AXES),
            P(AXES, None, None),
            P(),
            P(),
        ),
        out_specs=(table,) * 4,
        check_vma=False,
    )
```

```python
import functools

import jax
import jax.numpy as jnp
from jax import lax
from jax.experimental import pallas as pl
from jax.experimental.pallas import tpu as pltpu
from jax.sharding import PartitionSpec as P

LOG_TOTAL = 14.3
LEARN_RATE = 0.05
AXES = ("rows", "cols")
TILE = 256
VMEM_LIMIT = 60 * 1024 * 1024

BF16 = jnp.bfloat16
F32 = jnp.float32


def vmem_spec():
    return pl.BlockSpec(memory_space=pltpu.VMEM)


def params():
    return pltpu.CompilerParams(vmem_limit_bytes=VMEM_LIMIT)


def pick_kernel(req, row_ref, col_ref, out_ref, held, sems):
    nodes, lists = out_ref.shape[:2]
    chunks = sems.shape[0]
    span = nodes // chunks
    copies = []
    for chunk in range(chunks):

        def one(i, carry, base=chunk * span):
            node = base + i
            for k in range(0, lists, 2):
                held[node, k] = row_ref[req[node, k]]
                held[node, k + 1] = col_ref[req[node, k + 1]]
            return carry

        lax.fori_loop(0, span, one, 0)
        part = pl.ds(chunk * span, span)
        copy = pltpu.make_async_copy(held.at[part], out_ref.at[part], sems.at[chunk])
        copy.start()
        copies.append(copy)
    for copy in copies:
        copy.wait()


def pick(req, rows, cols):
    nodes, lists = req.shape
    piece, width = rows.shape[1:]
    return pl.pallas_call(
        pick_kernel,
        out_shape=jax.ShapeDtypeStruct((nodes, lists, piece, width), BF16),
        grid_spec=pltpu.PrefetchScalarGridSpec(
            num_scalar_prefetch=1,
            grid=(),
            in_specs=[vmem_spec()] * 2,
            out_specs=pl.BlockSpec(memory_space=pltpu.HBM),
            scratch_shapes=[
                pltpu.VMEM((nodes, lists, piece, width), BF16),
                pltpu.SemaphoreType.DMA((8,)),
            ],
        ),
        compiler_params=pltpu.CompilerParams(vmem_limit_bytes=16 * 1024 * 1024),
        cost_estimate=pl.CostEstimate(
            flops=0,
            bytes_accessed=4 * rows.size + nodes * lists * piece * width * 2,
            transcendentals=0,
        ),
        name="pick",
    )(req, rows, cols)


def item_kernel(first, pairs, live, rows_ref, cols_ref, *refs):
    *count_refs, rm_ref, cm_ref, out_ref = refs
    slot = first + pl.program_id(0)
    groups, _, piece, width = rows_ref.shape
    blk = groups * piece
    alive = slot < live[0]

    @pl.when(alive)
    def _():
        a = pairs[slot, 0]
        b = pairs[slot, 1]
        cols = cols_ref[...].reshape(blk, width)
        col_log = jnp.log(cm_ref[pl.ds(b, 1), :].astype(F32))
        scale = 1.0 / (blk**0.5)
        parts = []
        deltas = []
        for start, counts_ref in zip(range(0, blk, TILE), count_refs):
            span = slice(start // piece, (start + TILE) // piece)
            rows = rows_ref[span].reshape(TILE, width)
            logits = lax.dot_general(
                rows, cols, (((1,), (1,)), ((), ())), preferred_element_type=F32
            )
            row_log = jnp.log(rm_ref[pl.ds(a, 1), start : start + TILE].astype(F32)) - LOG_TOTAL
            row_log = jnp.transpose(jnp.broadcast_to(row_log, (8, TILE)))[:, :1]
            counts = counts_ref[0].astype(F32)
            seen = jnp.maximum(counts, 1.0)
            spread = ((logits + row_log) + col_log) - jnp.log(seen)
            weight = 0.1 * scale + (0.25 * scale) * (seen * lax.rsqrt(seen))
            unseen = (0.5 * scale) * jnp.tanh(0.5 * spread) + 0.5 * scale
            delta = jnp.where(counts > 0.0, weight * spread, unseen).astype(BF16)
            row_part = jnp.dot(delta, cols, preferred_element_type=F32).astype(BF16)
            out_ref[span, 0] = row_part.reshape(TILE // piece, piece, width)
            parts.append(rows)
            deltas.append(delta)
        col_part = lax.dot_general(
            jnp.concatenate(parts, 0),
            jnp.concatenate(deltas, 0),
            (((0,), (0,)), ((), ())),
            preferred_element_type=F32,
        )
        out_ref[:, 1] = jnp.transpose(col_part).astype(BF16).reshape(groups, piece, width)

    @pl.when(jnp.logical_not(alive))
    def _():
        out_ref[...] = jnp.zeros_like(out_ref)


def join(got):
    nodes, lists, piece, width = got.shape
    if piece % 16 == 0:
        return got
    got = got.transpose(1, 0, 2, 3).reshape(lists, nodes * piece // TILE, TILE, width)
    return got.transpose(1, 0, 2, 3)


def cut(out, nodes, piece):
    groups, lists, rows, width = out.shape
    if rows == piece:
        return out
    out = out.transpose(1, 0, 2, 3).reshape(lists, nodes, piece, width)
    return out.transpose(1, 0, 2, 3)


def items(pairs, live, got, counts, row_marginal, col_marginal, first, count):
    nodes, _, piece, width = got.shape
    blk = counts.shape[1]
    got = join(got)
    groups, lists, rows_in, _ = got.shape
    whole = pl.BlockSpec(row_marginal.shape, lambda s, *_: (0, 0))
    tiles = blk // TILE

    def table(k):
        return pl.BlockSpec((groups, 1, rows_in, width), lambda s, *_: (0, 2 * (first + s) + k, 0, 0))

    def chunk(i):
        return pl.BlockSpec((1, TILE, blk), lambda s, *_: (first + s, i, 0))

    out = pl.pallas_call(
        functools.partial(item_kernel, first),
        out_shape=jax.ShapeDtypeStruct((groups, 2 * count, rows_in, width), BF16),
        grid_spec=pltpu.PrefetchScalarGridSpec(
            num_scalar_prefetch=2,
            grid=(count,),
            in_specs=[
                table(0),
                table(1),
                *(chunk(i) for i in range(tiles)),
                whole,
                whole,
            ],
            out_specs=pl.BlockSpec((groups, 2, rows_in, width), lambda s, *_: (0, s, 0, 0)),
        ),
        compiler_params=params(),
        cost_estimate=pl.CostEstimate(
            flops=6 * count * blk * blk * width,
            bytes_accessed=count * (blk * blk * 4 + 4 * blk * width * 2),
            transcendentals=3 * count * blk * blk,
        ),
        name="items",
    )(pairs, live, got, got, *([counts] * tiles), row_marginal, col_marginal)
    return cut(out, nodes, piece)


def add_parts(first, req, ret_ref, row_acc, col_acc):
    def one(node, carry):
        for k in range(0, ret_ref.shape[1], 2):
            row_acc[req[node, first + k]] += ret_ref[node, k].astype(F32)
            col_acc[req[node, first + k + 1]] += ret_ref[node, k + 1].astype(F32)
        return carry

    lax.fori_loop(0, ret_ref.shape[0], one, 0)


def sum_kernel(req, ret_ref, row_out, col_out):
    row_out[...] = jnp.zeros_like(row_out)
    col_out[...] = jnp.zeros_like(col_out)
    add_parts(0, req, ret_ref, row_out, col_out)


def sums(req, ret, blocks):
    piece, width = ret.shape[2:]
    shape = jax.ShapeDtypeStruct((blocks, piece, width), F32)
    return pl.pallas_call(
        sum_kernel,
        out_shape=(shape, shape),
        grid_spec=pltpu.PrefetchScalarGridSpec(
            num_scalar_prefetch=1,
            in_specs=[vmem_spec()],
            out_specs=(vmem_spec(), vmem_spec()),
            grid=(),
        ),
        compiler_params=params(),
        cost_estimate=pl.CostEstimate(
            flops=ret.size,
            bytes_accessed=ret.size * 2 + 8 * blocks * piece * width,
            transcendentals=0,
        ),
        name="sums",
    )(req, ret)


def update_kernel(first, req, ret_ref, rg, cg, rm, ra, cm, ca, rn, ran, cn, can, row_s, col_s):
    row_s[...] = rg[...]
    col_s[...] = cg[...]
    add_parts(first, req, ret_ref, row_s, col_s)
    for grads, master, accum, new, accum_out in ((row_s, rm, ra, rn, ran), (col_s, cm, ca, cn, can)):
        grad = grads[...]
        accum_new = accum[...] + grad * grad
        accum_out[...] = accum_new
        new[...] = master[...] - LEARN_RATE * grad * lax.rsqrt(accum_new)


def update(req, ret, row_grad, col_grad, row_master, row_accum, col_master, col_accum, first):
    blocks, piece, width = row_master.shape
    nodes, lists = ret.shape[:2]
    shape = jax.ShapeDtypeStruct(row_master.shape, F32)
    rows = piece if piece % 16 else 16
    table = pl.BlockSpec((blocks, rows, width), lambda i, *_: (0, i, 0))
    return pl.pallas_call(
        functools.partial(update_kernel, first),
        out_shape=(shape,) * 4,
        grid_spec=pltpu.PrefetchScalarGridSpec(
            num_scalar_prefetch=1,
            grid=(piece // rows,),
            in_specs=[pl.BlockSpec((nodes, lists, rows, width), lambda i, *_: (0, 0, i, 0))]
            + [table] * 6,
            out_specs=(table,) * 4,
            scratch_shapes=[pltpu.VMEM((blocks, rows, width), F32)] * 2,
        ),
        compiler_params=params(),
        cost_estimate=pl.CostEstimate(
            flops=8 * row_master.size,
            bytes_accessed=ret.size * 2 + 40 * row_master.size,
            transcendentals=2 * row_master.size,
        ),
        name="update",
    )(req, ret, row_grad, col_grad, row_master, row_accum, col_master, col_accum)


def exchange(x):
    return lax.all_to_all(x, AXES, split_axis=0, concat_axis=0, tiled=True)


def body(
    row_master, row_accum, col_master, col_accum, pairs, live, counts, row_marginal, col_marginal
):
    slots = pairs.shape[0]
    blocks = row_master.shape[0]
    nodes = lax.axis_size(AXES)
    req = exchange(jnp.broadcast_to(pairs.reshape(1, 2 * slots), (nodes, 2 * slots)))
    got = exchange(pick(req, row_master.astype(BF16), col_master.astype(BF16)))
    lead = 1
    back = items(pairs, live, got, counts, row_marginal, col_marginal, 0, lead)
    back = exchange(back)
    rest = items(pairs, live, got, counts, row_marginal, col_marginal, lead, slots - lead)
    rest, back = lax.optimization_barrier((rest, back))
    rest = exchange(rest)
    row_grad, col_grad = sums(req, back, blocks)
    return update(
        req, rest, row_grad, col_grad, row_master, row_accum, col_master, col_accum, 2 * lead
    )


def solution(mesh):
    table = P(None, AXES, None)
    return jax.shard_map(
        body,
        mesh=mesh,
        in_specs=(
            table,
            table,
            table,
            table,
            P(AXES, None),
            P(AXES),
            P(AXES, None, None),
            P(),
            P(),
        ),
        out_specs=(table,) * 4,
        check_vma=False,
    )
```

```python
import functools

import jax
import jax.numpy as jnp
from jax import lax
from jax.experimental import pallas as pl
from jax.experimental.pallas import tpu as pltpu
from jax.sharding import PartitionSpec as P

LOG_TOTAL = 14.3
LEARN_RATE = 0.05
AXES = ("rows", "cols")
TILE = 256
VMEM_LIMIT = 65280 * 1024
TILE = 256

BF16 = jnp.bfloat16
F32 = jnp.float32


def vmem_spec():
    return pl.BlockSpec(memory_space=pltpu.VMEM)


def hbm_spec():
    return pl.BlockSpec(memory_space=pltpu.HBM)


def params():
    return pltpu.CompilerParams(vmem_limit_bytes=VMEM_LIMIT)


def pick_kernel(first, req, row_ref, col_ref, out_ref, held, sems):
    nodes, lists = out_ref.shape[:2]
    chunks = sems.shape[0]
    span = nodes // chunks
    copies = []
    for chunk in range(chunks):

        def one(i, carry, base=chunk * span):
            node = base + i
            for k in range(0, lists, 2):
                held[node, k] = row_ref[req[node, 2 * first + k]]
                held[node, k + 1] = col_ref[req[node, 2 * first + k + 1]]
            return carry

        lax.fori_loop(0, span, one, 0)
        part = pl.ds(chunk * span, span)
        copy = pltpu.make_async_copy(held.at[part], out_ref.at[part], sems.at[chunk])
        copy.start()
        copies.append(copy)
    for copy in copies:
        copy.wait()


def pick(req, rows, cols, first, count):
    nodes = req.shape[0]
    lists = 2 * count
    piece, width = rows.shape[1:]
    return pl.pallas_call(
        functools.partial(pick_kernel, first),
        out_shape=jax.ShapeDtypeStruct((nodes, lists, piece, width), BF16),
        grid_spec=pltpu.PrefetchScalarGridSpec(
            num_scalar_prefetch=1,
            grid=(),
            in_specs=[vmem_spec()] * 2,
            out_specs=hbm_spec(),
            scratch_shapes=[
                pltpu.VMEM((nodes, lists, piece, width), BF16),
                pltpu.SemaphoreType.DMA((8,)),
            ],
        ),
        compiler_params=pltpu.CompilerParams(vmem_limit_bytes=16 * 1024 * 1024),
        cost_estimate=pl.CostEstimate(
            flops=0,
            bytes_accessed=4 * rows.size + nodes * lists * piece * width * 2,
            transcendentals=0,
        ),
        name="pick",
    )(req, rows, cols)


def item_kernel(first, pairs, live, rows_ref, cols_ref, *refs):
    *count_refs, rm_ref, cm_ref, out_ref = refs
    slot = first + pl.program_id(0)
    groups, _, piece, width = rows_ref.shape
    blk = groups * piece
    alive = slot < live[0]

    @pl.when(alive)
    def _():
        a = pairs[slot, 0]
        b = pairs[slot, 1]
        cols = cols_ref[...].reshape(blk, width)
        col_log = jnp.log(cm_ref[pl.ds(b, 1), :].astype(F32))
        scale = 1.0 / (blk**0.5)
        parts = []
        deltas = []
        for start, counts_ref in zip(range(0, blk, TILE), count_refs):
            span = slice(start // piece, (start + TILE) // piece)
            rows = rows_ref[span].reshape(TILE, width)
            logits = lax.dot_general(
                rows, cols, (((1,), (1,)), ((), ())), preferred_element_type=F32
            )
            row_log = jnp.log(rm_ref[pl.ds(a, 1), start : start + TILE].astype(F32)) - LOG_TOTAL
            row_log = jnp.transpose(jnp.broadcast_to(row_log, (8, TILE)))[:, :1]
            counts = counts_ref[0].astype(F32)
            seen = jnp.maximum(counts, 1.0)
            spread = ((logits + row_log) + col_log) - jnp.log(seen)
            weight = 0.1 * scale + (0.25 * scale) * (seen * lax.rsqrt(seen))
            unseen = (0.5 * scale) * jnp.tanh(0.5 * spread) + 0.5 * scale
            delta = jnp.where(counts > 0.0, weight * spread, unseen).astype(BF16)
            row_part = jnp.dot(delta, cols, preferred_element_type=F32).astype(BF16)
            out_ref[span, 0] = row_part.reshape(TILE // piece, piece, width)
            parts.append(rows)
            deltas.append(delta)
        col_part = lax.dot_general(
            jnp.concatenate(parts, 0),
            jnp.concatenate(deltas, 0),
            (((0,), (0,)), ((), ())),
            preferred_element_type=F32,
        )
        out_ref[:, 1] = jnp.transpose(col_part).astype(BF16).reshape(groups, piece, width)

    @pl.when(jnp.logical_not(alive))
    def _():
        out_ref[...] = jnp.zeros_like(out_ref)


def join(got):
    nodes, lists, piece, width = got.shape
    if piece % 16 == 0:
        return got
    got = got.transpose(1, 0, 2, 3).reshape(lists, nodes * piece // TILE, TILE, width)
    return got.transpose(1, 0, 2, 3)


def cut(out, nodes, piece):
    groups, lists, rows, width = out.shape
    if rows == piece:
        return out
    out = out.transpose(1, 0, 2, 3).reshape(lists, nodes, piece, width)
    return out.transpose(1, 0, 2, 3)


def items(pairs, live, got, counts, row_marginal, col_marginal, first, count):
    nodes, _, piece, width = got.shape
    blk = counts.shape[1]
    got = join(got)
    groups, lists, rows_in, _ = got.shape
    whole = pl.BlockSpec(row_marginal.shape, lambda s, *_: (0, 0))
    tiles = blk // TILE

    def table(k):
        return pl.BlockSpec((groups, 1, rows_in, width), lambda s, *_: (0, 2 * s + k, 0, 0))

    def chunk(i):
        return pl.BlockSpec((1, TILE, blk), lambda s, *_: (first + s, i, 0))

    out = pl.pallas_call(
        functools.partial(item_kernel, first),
        out_shape=jax.ShapeDtypeStruct((groups, 2 * count, rows_in, width), BF16),
        grid_spec=pltpu.PrefetchScalarGridSpec(
            num_scalar_prefetch=2,
            grid=(count,),
            in_specs=[
                table(0),
                table(1),
                *(chunk(i) for i in range(tiles)),
                whole,
                whole,
            ],
            out_specs=pl.BlockSpec((groups, 2, rows_in, width), lambda s, *_: (0, s, 0, 0)),
        ),
        compiler_params=params(),
        cost_estimate=pl.CostEstimate(
            flops=6 * count * blk * blk * width,
            bytes_accessed=count * (blk * blk * 4 + 4 * blk * width * 2),
            transcendentals=3 * count * blk * blk,
        ),
        name="items",
    )(pairs, live, got, got, *([counts] * tiles), row_marginal, col_marginal)
    return cut(out, nodes, piece)


def add_parts(first, req, ret_ref, row_acc, col_acc):
    def one(node, carry):
        for k in range(0, ret_ref.shape[1], 2):
            row_acc[req[node, first + k]] += ret_ref[node, k].astype(F32)
            col_acc[req[node, first + k + 1]] += ret_ref[node, k + 1].astype(F32)
        return carry

    lax.fori_loop(0, ret_ref.shape[0], one, 0)


def sum_kernel(first, req, ret_ref, row_out, col_out):
    row_out[...] = jnp.zeros_like(row_out)
    col_out[...] = jnp.zeros_like(col_out)
    add_parts(2 * first, req, ret_ref, row_out, col_out)


def sums(req, ret, blocks, first):
    piece, width = ret.shape[2:]
    shape = jax.ShapeDtypeStruct((blocks, piece, width), F32)
    return pl.pallas_call(
        functools.partial(sum_kernel, first),
        out_shape=(shape, shape),
        grid_spec=pltpu.PrefetchScalarGridSpec(
            num_scalar_prefetch=1,
            in_specs=[vmem_spec()],
            out_specs=(vmem_spec(), vmem_spec()),
            grid=(),
        ),
        compiler_params=params(),
        cost_estimate=pl.CostEstimate(
            flops=ret.size,
            bytes_accessed=ret.size * 2 + 8 * blocks * piece * width,
            transcendentals=0,
        ),
        name="sums",
    )(req, ret)


def update_kernel(
    first, req, ret_hbm, rg, cg, rm, ra, cm, ca, rn, ran, cn, can, ret_ref, held, done, ret_sems, sems, out_sems
):
    lists = ret_hbm.shape[1]
    tables = ((rg, rm, ra, rn, ran), (cg, cm, ca, cn, can))
    parts, loads, stores = {}, {}, []
    for side, refs in enumerate(tables):
        for k in range(side, lists, 2):
            parts[k] = pltpu.make_async_copy(ret_hbm.at[:, k], ret_ref.at[k], ret_sems.at[k])
            parts[k].start()
        for i in range(3):
            at = 3 * side + i
            loads[at] = pltpu.make_async_copy(refs[i], held.at[at], sems.at[at])
            loads[at].start()
    for side, refs in enumerate(tables):
        at = 3 * side
        loads[at].wait()
        for k in range(side, lists, 2):
            parts[k].wait()

            def one(node, carry, k=k, at=at):
                held[at, req[node, 2 * first + k]] += ret_ref[k, node].astype(F32)
                return carry

            lax.fori_loop(0, ret_hbm.shape[0], one, 0, unroll=4)
        loads[at + 1].wait()
        loads[at + 2].wait()
        grad = held[at]
        accum_new = held[at + 2] + grad * grad
        done[2 * side + 1] = accum_new
        done[2 * side] = held[at + 1] - LEARN_RATE * grad * lax.rsqrt(accum_new)
        for i in range(2):
            copy = pltpu.make_async_copy(
                done.at[2 * side + i], refs[3 + i], out_sems.at[2 * side + i]
            )
            copy.start()
            stores.append(copy)
    for copy in stores:
        copy.wait()


def update(req, ret, row_grad, col_grad, row_master, row_accum, col_master, col_accum, first):
    shape = jax.ShapeDtypeStruct(row_master.shape, F32)
    return pl.pallas_call(
        functools.partial(update_kernel, first),
        out_shape=(shape,) * 4,
        grid_spec=pltpu.PrefetchScalarGridSpec(
            num_scalar_prefetch=1,
            grid=(),
            in_specs=[hbm_spec()] * 7,
            out_specs=(hbm_spec(),) * 4,
            scratch_shapes=[
                pltpu.VMEM((ret.shape[1], ret.shape[0]) + ret.shape[2:], BF16),
                pltpu.VMEM((6,) + row_master.shape, F32),
                pltpu.VMEM((4,) + row_master.shape, F32),
                pltpu.SemaphoreType.DMA((ret.shape[1],)),
                pltpu.SemaphoreType.DMA((6,)),
                pltpu.SemaphoreType.DMA((4,)),
            ],
        ),
        compiler_params=params(),
        cost_estimate=pl.CostEstimate(
            flops=8 * row_master.size,
            bytes_accessed=ret.size * 2 + 40 * row_master.size,
            transcendentals=2 * row_master.size,
        ),
        name="update",
    )(req, ret, row_grad, col_grad, row_master, row_accum, col_master, col_accum)


def exchange(x):
    return lax.all_to_all(x, AXES, split_axis=0, concat_axis=0, tiled=True)


def body(
    row_master, row_accum, col_master, col_accum, pairs, live, counts, row_marginal, col_marginal
):
    slots = pairs.shape[0]
    blocks = row_master.shape[0]
    nodes = lax.axis_size(AXES)
    req = exchange(jnp.broadcast_to(pairs.reshape(1, 2 * slots), (nodes, 2 * slots)))
    row_low = row_master.astype(BF16)
    col_low = col_master.astype(BF16)
    lists = ((1, slots - 1), (0, 1))
    got = [exchange(pick(req, row_low, col_low, *part)) for part in lists]
    back = []
    for part, rows in zip(lists, got):
        work = items(pairs, live, rows, counts, row_marginal, col_marginal, *part)
        if back:
            work, back[-1] = lax.optimization_barrier((work, back[-1]))
        back.append(exchange(work))
    row_grad, col_grad = sums(req, back[0], blocks, 1)
    return update(req, back[1], row_grad, col_grad, row_master, row_accum, col_master, col_accum, 0)


def solution(mesh):
    table = P(None, AXES, None)
    return jax.shard_map(
        body,
        mesh=mesh,
        in_specs=(
            table,
            table,
            table,
            table,
            P(AXES, None),
            P(AXES),
            P(AXES, None, None),
            P(),
            P(),
        ),
        out_specs=(table,) * 4,
        check_vma=False,
    )
```

```python
import functools

import jax
import jax.numpy as jnp
from jax import lax
from jax.experimental import pallas as pl
from jax.experimental.pallas import tpu as pltpu
from jax.sharding import PartitionSpec as P

LOG_TOTAL = 14.3
LEARN_RATE = 0.05
AXES = ("rows", "cols")
TILE = 512
JOINED = 256
VMEM_LIMIT = 65280 * 1024

BF16 = jnp.bfloat16
F32 = jnp.float32


def vmem_spec():
    return pl.BlockSpec(memory_space=pltpu.VMEM)


def hbm_spec():
    return pl.BlockSpec(memory_space=pltpu.HBM)


def params():
    return pltpu.CompilerParams(vmem_limit_bytes=VMEM_LIMIT)


def pick_kernel(first, req, row_ref, col_ref, out_ref, held, sems):
    nodes, lists = out_ref.shape[:2]
    chunks = sems.shape[0]
    span = nodes // chunks
    copies = []
    for chunk in range(chunks):

        def one(i, carry, base=chunk * span):
            node = base + i
            for k in range(0, lists, 2):
                held[node, k] = row_ref[req[node, 0, first + k // 2]]
                held[node, k + 1] = col_ref[req[node, 1, first + k // 2]]
            return carry

        lax.fori_loop(0, span, one, 0)
        part = pl.ds(chunk * span, span)
        copy = pltpu.make_async_copy(held.at[part], out_ref.at[part], sems.at[chunk])
        copy.start()
        copies.append(copy)
    for copy in copies:
        copy.wait()


def pick(req, rows, cols, first, count):
    nodes = req.shape[0]
    lists = 2 * count
    piece, width = rows.shape[1:]
    return pl.pallas_call(
        functools.partial(pick_kernel, first),
        out_shape=jax.ShapeDtypeStruct((nodes, lists, piece, width), BF16),
        grid_spec=pltpu.PrefetchScalarGridSpec(
            num_scalar_prefetch=1,
            grid=(),
            in_specs=[vmem_spec()] * 2,
            out_specs=hbm_spec(),
            scratch_shapes=[
                pltpu.VMEM((nodes, lists, piece, width), BF16),
                pltpu.SemaphoreType.DMA((8,)),
            ],
        ),
        compiler_params=pltpu.CompilerParams(vmem_limit_bytes=VMEM_LIMIT if first else VMEM_LIMIT // 4),
        cost_estimate=pl.CostEstimate(
            flops=0,
            bytes_accessed=4 * rows.size + nodes * lists * piece * width * 2,
            transcendentals=0,
        ),
        name="pick",
    )(req, rows, cols)


def prepare_kernel(pairs, live, counts_ref, rm_ref, cm_ref, bias_ref, weight_ref):
    slot = pl.program_id(0)
    size, blk = counts_ref.shape[1:]

    @pl.when(slot < live[0])
    def _():
        at = pl.multiple_of(pl.program_id(1) * size, size)
        col_log = jnp.log(cm_ref[pl.ds(pairs[slot, 1], 1), :].astype(F32))
        row_log = jnp.log(rm_ref[pl.ds(pairs[slot, 0], 1), pl.ds(at, size)].astype(F32)) - LOG_TOTAL
        row_log = jnp.transpose(jnp.broadcast_to(row_log, (8, size)))[:, :1]
        scale = 1.0 / (blk**0.5)
        counts = counts_ref[0].astype(F32)
        seen = jnp.maximum(counts, 1.0)
        bias_ref[0] = (row_log + col_log) - jnp.log(seen)
        weight = 0.1 * scale + (0.25 * scale) * (seen * lax.rsqrt(seen))
        weight_ref[0] = jnp.where(counts > 0.0, weight, 0.0)


def prepare(pairs, live, counts, row_marginal, col_marginal):
    slots, blk, _ = counts.shape
    size = blk // 4
    tile = pl.BlockSpec((1, size, blk), lambda s, i, *_: (s, i, 0))
    whole = pl.BlockSpec(row_marginal.shape, lambda s, i, *_: (0, 0))
    shape = jax.ShapeDtypeStruct(counts.shape, F32)
    return pl.pallas_call(
        prepare_kernel,
        out_shape=(shape, shape),
        grid_spec=pltpu.PrefetchScalarGridSpec(
            num_scalar_prefetch=2,
            grid=(slots, blk // size),
            in_specs=[tile, whole, whole],
            out_specs=(tile, tile),
        ),
        compiler_params=params(),
        cost_estimate=pl.CostEstimate(
            flops=10 * counts.size, bytes_accessed=12 * counts.size, transcendentals=2 * counts.size
        ),
        name="prepare",
    )(pairs, live, counts, row_marginal, col_marginal)


def item_kernel(first, live, rows_ref, cols_ref, bias_ref, weight_ref, *refs):
    out_ref, acc_s = refs[-2:]
    slot = first + pl.program_id(0)
    step = pl.program_id(1)
    groups, _, piece, width = rows_ref.shape
    blk = groups * piece
    span = TILE // piece
    alive = slot < live[0]

    @pl.when(alive)
    def _():
        cols = cols_ref[...].reshape(blk, width)
        rows = rows_ref[pl.ds(step * span, span)].reshape(TILE, width)
        logits = lax.dot_general(rows, cols, (((1,), (1,)), ((), ())), preferred_element_type=F32)
        spread = logits + bias_ref[0]
        weight = weight_ref[0]
        scale = 1.0 / (blk**0.5)
        unseen = (0.5 * scale) * jnp.tanh(0.5 * spread) + 0.5 * scale
        delta = jnp.where(weight > 0.0, weight * spread, unseen).astype(BF16)
        row_part = jnp.dot(delta, cols, preferred_element_type=F32).astype(BF16)
        out_ref[pl.ds(step * span, span), 0] = row_part.reshape(span, piece, width)
        part = lax.dot_general(rows, delta, (((0,), (0,)), ((), ())), preferred_element_type=F32)

        @pl.when(step == 0)
        def _():
            acc_s[...] = part

        @pl.when(step == pl.num_programs(1) - 1)
        def _():
            total = jnp.transpose(acc_s[...] + part)
            out_ref[:, 1] = total.astype(BF16).reshape(groups, piece, width)

    @pl.when(jnp.logical_not(alive) & (step == 0))
    def _():
        out_ref[...] = jnp.zeros_like(out_ref)


def join(got):
    nodes, lists, piece, width = got.shape
    if piece % 16 == 0:
        return got
    got = got.transpose(1, 0, 2, 3).reshape(lists, nodes * piece // JOINED, JOINED, width)
    return got.transpose(1, 0, 2, 3)


def cut(out, nodes, piece):
    groups, lists, rows, width = out.shape
    if rows == piece:
        return out
    out = out.transpose(1, 0, 2, 3).reshape(lists, nodes, piece, width)
    return out.transpose(1, 0, 2, 3)


def items(live, got, bias, weight, first, count, into=None):
    width = got.shape[3]
    slots, blk, _ = bias.shape
    got = join(got)
    groups, _, rows_in, _ = got.shape
    steps = blk // TILE
    assert steps == 2

    def table(k):
        return pl.BlockSpec((groups, 1, rows_in, width), lambda s, i, *_: (0, 2 * s + k, 0, 0))

    tile = pl.BlockSpec((1, TILE, blk), lambda s, i, *_: (first + s, i, 0))
    earlier = () if into is None else (into,)
    return pl.pallas_call(
        functools.partial(item_kernel, first),
        out_shape=jax.ShapeDtypeStruct((groups, 2 * slots, rows_in, width), BF16),
        grid_spec=pltpu.PrefetchScalarGridSpec(
            num_scalar_prefetch=1,
            grid=(count, steps),
            in_specs=[table(0), table(1), tile, tile] + [hbm_spec()] * len(earlier),
            out_specs=pl.BlockSpec((groups, 2, rows_in, width), lambda s, i, *_: (0, first + s, 0, 0)),
            scratch_shapes=[pltpu.VMEM((width, blk), F32)],
        ),
        input_output_aliases={5: 0} if earlier else {},
        compiler_params=params(),
        cost_estimate=pl.CostEstimate(
            flops=6 * count * blk * blk * width,
            bytes_accessed=count * (blk * blk * 8 + 4 * blk * width * 2),
            transcendentals=count * blk * blk,
        ),
        name="items",
    )(live, got, got, bias, weight, *earlier)


def update_kernel(req, ret_hbm, rm, ra, cm, ca, rn, ran, cn, can, ret_ref, grads, held, done, ret_sems, sems, out_sems):
    lists = ret_hbm.shape[1]
    tables = ((rm, ra, rn, ran), (cm, ca, cn, can))
    parts, loads, stores = {}, {}, []
    for side, refs in enumerate(tables):
        for k in range(side, lists, 2):
            parts[k] = pltpu.make_async_copy(ret_hbm.at[:, k], ret_ref.at[k], ret_sems.at[k])
            parts[k].start()
        for i in range(2):
            at = 2 * side + i
            loads[at] = pltpu.make_async_copy(refs[i], held.at[at], sems.at[at])
            loads[at].start()
    grads[...] = jnp.zeros_like(grads)
    for side, refs in enumerate(tables):
        for k in range(side, lists, 2):
            parts[k].wait()

            def one(node, carry, k=k, side=side):
                grads[side, req[node, side, k // 2]] += ret_ref[k, node].astype(F32)
                return carry

            lax.fori_loop(0, ret_hbm.shape[0], one, 0, unroll=4)
        at = 2 * side
        loads[at].wait()
        loads[at + 1].wait()
        grad = grads[side]
        accum_new = held[at + 1] + grad * grad
        done[at + 1] = accum_new
        done[at] = held[at] - LEARN_RATE * grad * lax.rsqrt(accum_new)
        for i in range(2):
            copy = pltpu.make_async_copy(done.at[at + i], refs[2 + i], out_sems.at[at + i])
            copy.start()
            stores.append(copy)
    for copy in stores:
        copy.wait()


def update(req, ret, row_master, row_accum, col_master, col_accum):
    shape = jax.ShapeDtypeStruct(row_master.shape, F32)
    nodes, lists = ret.shape[:2]
    return pl.pallas_call(
        update_kernel,
        out_shape=(shape,) * 4,
        grid_spec=pltpu.PrefetchScalarGridSpec(
            num_scalar_prefetch=1,
            grid=(),
            in_specs=[hbm_spec()] * 5,
            out_specs=(hbm_spec(),) * 4,
            scratch_shapes=[
                pltpu.VMEM((lists, nodes) + ret.shape[2:], BF16),
                pltpu.VMEM((2,) + row_master.shape, F32),
                pltpu.VMEM((4,) + row_master.shape, F32),
                pltpu.VMEM((4,) + row_master.shape, F32),
                pltpu.SemaphoreType.DMA((lists,)),
                pltpu.SemaphoreType.DMA((4,)),
                pltpu.SemaphoreType.DMA((4,)),
            ],
        ),
        compiler_params=params(),
        cost_estimate=pl.CostEstimate(
            flops=8 * row_master.size + ret.size,
            bytes_accessed=ret.size * 2 + 32 * row_master.size,
            transcendentals=2 * row_master.size,
        ),
        name="update",
    )(req, ret, row_master, row_accum, col_master, col_accum)


def exchange(x):
    return lax.all_to_all(x, AXES, split_axis=0, concat_axis=0, tiled=True)


def body(
    row_master, row_accum, col_master, col_accum, pairs, live, counts, row_marginal, col_marginal
):
    slots = pairs.shape[0]
    nodes = lax.axis_size(AXES)
    req = exchange(jnp.broadcast_to(pairs.T[None], (nodes, 2, slots)))
    row_low = row_master.astype(BF16)
    col_low = col_master.astype(BF16)
    last = slots - 1
    first_got = exchange(pick(req, row_low, col_low, 0, last))
    bias, weight = prepare(pairs, live, counts, row_marginal, col_marginal)
    picked = pick(req, row_low, col_low, last, 1)
    picked, bias, weight = lax.optimization_barrier((picked, bias, weight))
    last_got = exchange(picked)
    parts = items(live, first_got, bias, weight, 0, last)
    parts = items(live, last_got, bias, weight, last, 1, parts)
    back = exchange(cut(parts, nodes, row_master.shape[1]))
    return update(req, back, row_master, row_accum, col_master, col_accum)


def solution(mesh):
    table = P(None, AXES, None)
    return jax.shard_map(
        body,
        mesh=mesh,
        in_specs=(
            table,
            table,
            table,
            table,
            P(AXES, None),
            P(AXES),
            P(AXES, None, None),
            P(),
            P(),
        ),
        out_specs=(table,) * 4,
        check_vma=False,
    )
```

```python
import functools

import jax
import jax.numpy as jnp
from jax import lax
from jax.experimental import pallas as pl
from jax.experimental.pallas import tpu as pltpu
from jax.sharding import PartitionSpec as P

LOG_TOTAL = 14.3
LEARN_RATE = 0.05
AXES = ("rows", "cols")
TILE = 512
JOINED = 256
VMEM_LIMIT = 65280 * 1024

BF16 = jnp.bfloat16
F32 = jnp.float32


def vmem_spec():
    return pl.BlockSpec(memory_space=pltpu.VMEM)


def hbm_spec():
    return pl.BlockSpec(memory_space=pltpu.HBM)


def params():
    return pltpu.CompilerParams(vmem_limit_bytes=VMEM_LIMIT)


def pick_kernel(first, req, row_ref, col_ref, out_ref, held, sems):
    nodes, lists = out_ref.shape[:2]
    chunks = sems.shape[0]
    span = nodes // chunks
    copies = []
    for chunk in range(chunks):

        def one(i, carry, base=chunk * span):
            node = base + i
            for k in range(0, lists, 2):
                held[node, k] = row_ref[req[node, 0, first + k // 2]]
                held[node, k + 1] = col_ref[req[node, 1, first + k // 2]]
            return carry

        lax.fori_loop(0, span, one, 0)
        part = pl.ds(chunk * span, span)
        copy = pltpu.make_async_copy(held.at[part], out_ref.at[part], sems.at[chunk])
        copy.start()
        copies.append(copy)
    for copy in copies:
        copy.wait()


def pick(req, rows, cols, first, count):
    nodes = req.shape[0]
    lists = 2 * count
    piece, width = rows.shape[1:]
    return pl.pallas_call(
        functools.partial(pick_kernel, first),
        out_shape=jax.ShapeDtypeStruct((nodes, lists, piece, width), BF16),
        grid_spec=pltpu.PrefetchScalarGridSpec(
            num_scalar_prefetch=1,
            grid=(),
            in_specs=[vmem_spec()] * 2,
            out_specs=hbm_spec(),
            scratch_shapes=[
                pltpu.VMEM((nodes, lists, piece, width), BF16),
                pltpu.SemaphoreType.DMA((8,)),
            ],
        ),
        compiler_params=pltpu.CompilerParams(vmem_limit_bytes=VMEM_LIMIT if first else VMEM_LIMIT // 4),
        cost_estimate=pl.CostEstimate(
            flops=0,
            bytes_accessed=4 * rows.size + nodes * lists * piece * width * 2,
            transcendentals=0,
        ),
        name="pick",
    )(req, rows, cols)


def prepare_kernel(slot, pairs, live, counts_ref, rm_ref, cm_ref, bias_ref, weight_ref):
    size, blk = counts_ref.shape[1:]

    @pl.when(slot < live[0])
    def _():
        at = pl.multiple_of(pl.program_id(0) * size, size)
        col_log = jnp.log(cm_ref[pl.ds(pairs[slot, 1], 1), :].astype(F32))
        row_log = jnp.log(rm_ref[pl.ds(pairs[slot, 0], 1), pl.ds(at, size)].astype(F32)) - LOG_TOTAL
        row_log = jnp.transpose(jnp.broadcast_to(row_log, (8, size)))[:, :1]
        scale = 1.0 / (blk**0.5)
        counts = counts_ref[0].astype(F32)
        seen = jnp.maximum(counts, 1.0)
        bias_ref[0] = (row_log + col_log) - jnp.log(seen)
        weight = 0.1 * scale + (0.25 * scale) * (seen * lax.rsqrt(seen))
        weight_ref[0] = jnp.where(counts > 0.0, weight, 0.0)


def prepare(pairs, live, counts, row_marginal, col_marginal, slot):
    _, blk, _ = counts.shape
    size = blk // 4
    tile = pl.BlockSpec((1, size, blk), lambda i, *_: (slot, i, 0))
    ready = pl.BlockSpec((1, size, blk), lambda i, *_: (0, i, 0))
    whole = pl.BlockSpec(row_marginal.shape, lambda i, *_: (0, 0))
    shape = jax.ShapeDtypeStruct((1, blk, blk), F32)
    return pl.pallas_call(
        functools.partial(prepare_kernel, slot),
        out_shape=(shape, shape),
        grid_spec=pltpu.PrefetchScalarGridSpec(
            num_scalar_prefetch=2,
            grid=(blk // size,),
            in_specs=[tile, whole, whole],
            out_specs=(ready, ready),
        ),
        compiler_params=params(),
        cost_estimate=pl.CostEstimate(
            flops=10 * blk * blk, bytes_accessed=12 * blk * blk, transcendentals=2 * blk * blk
        ),
        name="prepare",
    )(pairs, live, counts, row_marginal, col_marginal)


def early_kernel(first, pairs, live, rows_ref, cols_ref, *refs):
    *count_refs, rm_ref, cm_ref, out_ref = refs
    slot = first + pl.program_id(0)
    groups, _, piece, width = rows_ref.shape
    blk = groups * piece
    alive = slot < live[0]

    @pl.when(alive)
    def _():
        a = pairs[slot, 0]
        b = pairs[slot, 1]
        cols = cols_ref[...].reshape(blk, width)
        col_log = jnp.log(cm_ref[pl.ds(b, 1), :].astype(F32))
        scale = 1.0 / (blk**0.5)
        parts = []
        deltas = []
        for start, counts_ref in zip(range(0, blk, JOINED), count_refs):
            span = slice(start // piece, (start + JOINED) // piece)
            rows = rows_ref[span].reshape(JOINED, width)
            logits = lax.dot_general(
                rows, cols, (((1,), (1,)), ((), ())), preferred_element_type=F32
            )
            row_log = jnp.log(rm_ref[pl.ds(a, 1), start : start + JOINED].astype(F32)) - LOG_TOTAL
            row_log = jnp.transpose(jnp.broadcast_to(row_log, (8, JOINED)))[:, :1]
            counts = counts_ref[0].astype(F32)
            seen = jnp.maximum(counts, 1.0)
            spread = ((logits + row_log) + col_log) - jnp.log(seen)
            weight = 0.1 * scale + (0.25 * scale) * (seen * lax.rsqrt(seen))
            unseen = (0.5 * scale) * jnp.tanh(0.5 * spread) + 0.5 * scale
            delta = jnp.where(counts > 0.0, weight * spread, unseen).astype(BF16)
            row_part = jnp.dot(delta, cols, preferred_element_type=F32).astype(BF16)
            out_ref[span, 0] = row_part.reshape(JOINED // piece, piece, width)
            parts.append(rows)
            deltas.append(delta)
        col_part = lax.dot_general(
            jnp.concatenate(parts, 0),
            jnp.concatenate(deltas, 0),
            (((0,), (0,)), ((), ())),
            preferred_element_type=F32,
        )
        out_ref[:, 1] = jnp.transpose(col_part).astype(BF16).reshape(groups, piece, width)

    @pl.when(jnp.logical_not(alive))
    def _():
        out_ref[...] = jnp.zeros_like(out_ref)


def item_kernel(first, live, rows_ref, cols_ref, bias_ref, weight_ref, *refs):
    out_ref, acc_s = refs[-2:]
    slot = first + pl.program_id(0)
    step = pl.program_id(1)
    groups, _, piece, width = rows_ref.shape
    blk = groups * piece
    span = TILE // piece
    alive = slot < live[0]

    @pl.when(alive)
    def _():
        cols = cols_ref[...].reshape(blk, width)
        rows = rows_ref[pl.ds(step * span, span)].reshape(TILE, width)
        logits = lax.dot_general(rows, cols, (((1,), (1,)), ((), ())), preferred_element_type=F32)
        spread = logits + bias_ref[0]
        weight = weight_ref[0]
        scale = 1.0 / (blk**0.5)
        unseen = (0.5 * scale) * jnp.tanh(0.5 * spread) + 0.5 * scale
        delta = jnp.where(weight > 0.0, weight * spread, unseen).astype(BF16)
        row_part = jnp.dot(delta, cols, preferred_element_type=F32).astype(BF16)
        out_ref[pl.ds(step * span, span), 0] = row_part.reshape(span, piece, width)
        part = lax.dot_general(rows, delta, (((0,), (0,)), ((), ())), preferred_element_type=F32)

        @pl.when(step == 0)
        def _():
            acc_s[...] = part

        @pl.when(step == pl.num_programs(1) - 1)
        def _():
            total = jnp.transpose(acc_s[...] + part)
            out_ref[:, 1] = total.astype(BF16).reshape(groups, piece, width)

    @pl.when(jnp.logical_not(alive) & (step == 0))
    def _():
        out_ref[...] = jnp.zeros_like(out_ref)


def join(got):
    nodes, lists, piece, width = got.shape
    if piece % 16 == 0:
        return got
    got = got.transpose(1, 0, 2, 3).reshape(lists, nodes * piece // JOINED, JOINED, width)
    return got.transpose(1, 0, 2, 3)


def cut(out, nodes, piece):
    groups, lists, rows, width = out.shape
    if rows == piece:
        return out
    out = out.transpose(1, 0, 2, 3).reshape(lists, nodes, piece, width)
    return out.transpose(1, 0, 2, 3)


def early_items(pairs, live, got, counts, row_marginal, col_marginal, first, count):
    width = got.shape[3]
    blk = counts.shape[1]
    got = join(got)
    groups, lists, rows_in, _ = got.shape
    whole = pl.BlockSpec(row_marginal.shape, lambda s, *_: (0, 0))
    tiles = blk // JOINED

    def table(k):
        return pl.BlockSpec((groups, 1, rows_in, width), lambda s, *_: (0, 2 * s + k, 0, 0))

    def chunk(i):
        return pl.BlockSpec((1, JOINED, blk), lambda s, *_: (first + s, i, 0))

    out = pl.pallas_call(
        functools.partial(early_kernel, first),
        out_shape=jax.ShapeDtypeStruct((groups, 2 * counts.shape[0], rows_in, width), BF16),
        grid_spec=pltpu.PrefetchScalarGridSpec(
            num_scalar_prefetch=2,
            grid=(count,),
            in_specs=[
                table(0),
                table(1),
                *(chunk(i) for i in range(tiles)),
                whole,
                whole,
            ],
            out_specs=pl.BlockSpec((groups, 2, rows_in, width), lambda s, *_: (0, s, 0, 0)),
        ),
        compiler_params=params(),
        cost_estimate=pl.CostEstimate(
            flops=6 * count * blk * blk * width,
            bytes_accessed=count * (blk * blk * 4 + 4 * blk * width * 2),
            transcendentals=3 * count * blk * blk,
        ),
        name="early_items",
    )(pairs, live, got, got, *([counts] * tiles), row_marginal, col_marginal)
    return out


def items(live, got, bias, weight, first, count, into=None):
    width = got.shape[3]
    blk = bias.shape[1]
    slots = first + count
    got = join(got)
    groups, _, rows_in, _ = got.shape
    steps = blk // TILE
    assert steps == 2

    def table(k):
        return pl.BlockSpec((groups, 1, rows_in, width), lambda s, i, *_: (0, 2 * s + k, 0, 0))

    tile = pl.BlockSpec((1, TILE, blk), lambda s, i, *_: (s, i, 0))
    earlier = () if into is None else (into,)
    return pl.pallas_call(
        functools.partial(item_kernel, first),
        out_shape=jax.ShapeDtypeStruct((groups, 2 * slots, rows_in, width), BF16),
        grid_spec=pltpu.PrefetchScalarGridSpec(
            num_scalar_prefetch=1,
            grid=(count, steps),
            in_specs=[table(0), table(1), tile, tile] + [hbm_spec()] * len(earlier),
            out_specs=pl.BlockSpec((groups, 2, rows_in, width), lambda s, i, *_: (0, first + s, 0, 0)),
            scratch_shapes=[pltpu.VMEM((width, blk), F32)],
        ),
        input_output_aliases={5: 0} if earlier else {},
        compiler_params=params(),
        cost_estimate=pl.CostEstimate(
            flops=6 * count * blk * blk * width,
            bytes_accessed=count * (blk * blk * 8 + 4 * blk * width * 2),
            transcendentals=count * blk * blk,
        ),
        name="items",
    )(live, got, got, bias, weight, *earlier)


def update_kernel(req, ret_ref, rm, ra, cm, ca, rn, ran, cn, can, grads, done, out_sems):
    nodes, lists = ret_ref.shape[:2]
    tables = ((rm, ra, rn, ran), (cm, ca, cn, can))
    stores = []
    grads[...] = jnp.zeros_like(grads)
    for side, refs in enumerate(tables):
        for k in range(side, lists, 2):

            def one(node, carry, k=k, side=side):
                grads[side, req[node, side, k // 2]] += ret_ref[node, k].astype(F32)
                return carry

            lax.fori_loop(0, nodes, one, 0, unroll=4)
        at = 2 * side
        grad = grads[side]
        accum_new = refs[1][...] + grad * grad
        done[at + 1] = accum_new
        done[at] = refs[0][...] - LEARN_RATE * grad * lax.rsqrt(accum_new)
        for i in range(2):
            copy = pltpu.make_async_copy(done.at[at + i], refs[2 + i], out_sems.at[at + i])
            copy.start()
            stores.append(copy)
    for copy in stores:
        copy.wait()


def update(req, ret, row_master, row_accum, col_master, col_accum):
    shape = jax.ShapeDtypeStruct(row_master.shape, F32)
    return pl.pallas_call(
        update_kernel,
        out_shape=(shape,) * 4,
        grid_spec=pltpu.PrefetchScalarGridSpec(
            num_scalar_prefetch=1,
            grid=(),
            in_specs=[vmem_spec()] * 5,
            out_specs=(hbm_spec(),) * 4,
            scratch_shapes=[
                pltpu.VMEM((2,) + row_master.shape, F32),
                pltpu.VMEM((4,) + row_master.shape, F32),
                pltpu.SemaphoreType.DMA((4,)),
            ],
        ),
        compiler_params=pltpu.CompilerParams(vmem_limit_bytes=VMEM_LIMIT // 4),
        cost_estimate=pl.CostEstimate(
            flops=8 * row_master.size + ret.size,
            bytes_accessed=ret.size * 2 + 32 * row_master.size,
            transcendentals=2 * row_master.size,
        ),
        name="update",
    )(req, ret, row_master, row_accum, col_master, col_accum)


def exchange(x):
    return lax.all_to_all(x, AXES, split_axis=0, concat_axis=0, tiled=True)


def body(
    row_master, row_accum, col_master, col_accum, pairs, live, counts, row_marginal, col_marginal
):
    slots = pairs.shape[0]
    nodes = lax.axis_size(AXES)
    req = exchange(jnp.broadcast_to(pairs.T[None], (nodes, 2, slots)))
    row_low = row_master.astype(BF16)
    col_low = col_master.astype(BF16)
    last = slots - 1
    first_got = exchange(pick(req, row_low, col_low, 0, last))
    bias, weight = prepare(pairs, live, counts, row_marginal, col_marginal, last)
    picked = pick(req, row_low, col_low, last, 1)
    picked, bias, weight = lax.optimization_barrier((picked, bias, weight))
    last_got = exchange(picked)
    parts = early_items(pairs, live, first_got, counts, row_marginal, col_marginal, 0, last)
    parts = items(live, last_got, bias, weight, last, 1, parts)
    back = exchange(cut(parts, nodes, row_master.shape[1]))
    return update(req, back, row_master, row_accum, col_master, col_accum)


def solution(mesh):
    table = P(None, AXES, None)
    return jax.shard_map(
        body,
        mesh=mesh,
        in_specs=(
            table,
            table,
            table,
            table,
            P(AXES, None),
            P(AXES),
            P(AXES, None, None),
            P(),
            P(),
        ),
        out_specs=(table,) * 4,
        check_vma=False,
    )
```

```python
import functools

import jax
import jax.numpy as jnp
from jax import lax
from jax.experimental import pallas as pl
from jax.experimental.pallas import tpu as pltpu
from jax.sharding import PartitionSpec as P

LOG_TOTAL = 14.3
LEARN_RATE = 0.05
AXES = ("rows", "cols")
TILE = 512
JOINED = 256
VMEM_LIMIT = 65280 * 1024

BF16 = jnp.bfloat16
F32 = jnp.float32


def vmem_spec():
    return pl.BlockSpec(memory_space=pltpu.VMEM)


def hbm_spec():
    return pl.BlockSpec(memory_space=pltpu.HBM)


def params():
    return pltpu.CompilerParams(vmem_limit_bytes=VMEM_LIMIT)


def pick_kernel(first, req, pairs, live, row_ref, col_ref, out_ref, held, sems):
    nodes, lists = out_ref.shape[:2]
    chunks = sems.shape[0]
    span = nodes // chunks
    copies = []
    for chunk in range(chunks):

        def one(i, carry, base=chunk * span):
            node = base + i
            for k in range(0, lists, 2):
                held[node, k] = row_ref[req[node, 0, first + k // 2]]
                held[node, k + 1] = col_ref[req[node, 1, first + k // 2]]
            return carry

        lax.fori_loop(0, span, one, 0)
        part = pl.ds(chunk * span, span)
        copy = pltpu.make_async_copy(held.at[part], out_ref.at[part], sems.at[chunk])
        copy.start()
        copies.append(copy)
    for copy in copies:
        copy.wait()


def pick(req, pairs, live, rows, cols, first, count):
    nodes = req.shape[0]
    lists = 2 * count
    piece, width = rows.shape[1:]
    return pl.pallas_call(
        functools.partial(pick_kernel, first),
        out_shape=jax.ShapeDtypeStruct((nodes, lists, piece, width), BF16),
        grid_spec=pltpu.PrefetchScalarGridSpec(
            num_scalar_prefetch=3,
            grid=(),
            in_specs=[vmem_spec()] * 2,
            out_specs=hbm_spec(),
            scratch_shapes=[
                pltpu.VMEM((nodes, lists, piece, width), BF16),
                pltpu.SemaphoreType.DMA((8,)),
            ],
        ),
        compiler_params=pltpu.CompilerParams(vmem_limit_bytes=VMEM_LIMIT if first else VMEM_LIMIT // 4),
        cost_estimate=pl.CostEstimate(
            flops=0,
            bytes_accessed=4 * rows.size + nodes * lists * piece * width * 2,
            transcendentals=0,
        ),
        name="pick",
    )(req, pairs, live, rows, cols)


def item_kernel(pairs, live, got_ref, *refs):
    *count_refs, rm_ref, cm_ref, out_ref = refs
    slot = pl.program_id(0)
    groups, _, piece, width = got_ref.shape
    blk = groups * piece
    alive = slot < live[0]

    @pl.when(alive)
    def _():
        a = pairs[slot, 0]
        b = pairs[slot, 1]
        cols = got_ref[:, 2 * slot + 1].reshape(blk, width)
        col_log = jnp.log(cm_ref[pl.ds(b, 1), :].astype(F32))
        scale = 1.0 / (blk**0.5)
        parts = []
        deltas = []
        for start, counts_ref in zip(range(0, blk, TILE), count_refs):
            span = slice(start // piece, (start + TILE) // piece)
            rows = got_ref[span, 2 * slot].reshape(TILE, width)
            logits = lax.dot_general(
                rows, cols, (((1,), (1,)), ((), ())), preferred_element_type=F32
            )
            row_log = jnp.log(rm_ref[pl.ds(a, 1), start : start + TILE].astype(F32)) - LOG_TOTAL
            row_log = jnp.transpose(jnp.broadcast_to(row_log, (8, TILE)))[:, :1]
            counts = counts_ref[0].astype(F32)
            seen = jnp.maximum(counts, 1.0)
            spread = ((logits + row_log) + col_log) - jnp.log(seen)
            weight = 0.1 * scale + (0.25 * scale) * (seen * lax.rsqrt(seen))
            unseen = (0.5 * scale) * jnp.tanh(0.5 * spread) + 0.5 * scale
            delta = jnp.where(counts > 0.0, weight * spread, unseen).astype(BF16)
            row_part = jnp.dot(delta, cols, preferred_element_type=F32).astype(BF16)
            out_ref[span, 2 * slot] = row_part.reshape(TILE // piece, piece, width)
            parts.append(rows)
            deltas.append(delta)
        col_part = lax.dot_general(
            jnp.concatenate(parts, 0),
            jnp.concatenate(deltas, 0),
            (((0,), (0,)), ((), ())),
            preferred_element_type=F32,
        )
        out_ref[:, 2 * slot + 1] = jnp.transpose(col_part).astype(BF16).reshape(groups, piece, width)

    @pl.when(jnp.logical_not(alive))
    def _():
        for side in range(2):
            out_ref[:, 2 * slot + side] = jnp.zeros((groups, piece, width), BF16)


def join(got):
    nodes, lists, piece, width = got.shape
    if piece % 16 == 0:
        return got
    got = got.transpose(1, 0, 2, 3).reshape(lists, nodes * piece // JOINED, JOINED, width)
    return got.transpose(1, 0, 2, 3)


def cut(out, nodes, piece):
    groups, lists, rows, width = out.shape
    if rows == piece:
        return out
    out = out.transpose(1, 0, 2, 3).reshape(lists, nodes, piece, width)
    return out.transpose(1, 0, 2, 3)


def items(pairs, live, got, counts, row_marginal, col_marginal):
    nodes, _, piece, width = got.shape
    count, blk, _ = counts.shape
    got = join(got)
    tiles = blk // TILE

    def chunk(i):
        return pl.BlockSpec((1, TILE, blk), lambda s, *_: (s, i, 0))

    out = pl.pallas_call(
        item_kernel,
        out_shape=jax.ShapeDtypeStruct(got.shape, BF16),
        grid_spec=pltpu.PrefetchScalarGridSpec(
            num_scalar_prefetch=2,
            grid=(count,),
            in_specs=[vmem_spec(), *(chunk(i) for i in range(tiles)), vmem_spec(), vmem_spec()],
            out_specs=vmem_spec(),
        ),
        compiler_params=pltpu.CompilerParams(vmem_limit_bytes=VMEM_LIMIT * 5 // 8),
        cost_estimate=pl.CostEstimate(
            flops=6 * count * blk * blk * width,
            bytes_accessed=count * (blk * blk * 4 + 4 * blk * width * 2),
            transcendentals=3 * count * blk * blk,
        ),
        name="items",
    )(pairs, live, got, *([counts] * tiles), row_marginal, col_marginal)
    return cut(out, nodes, piece)


def update_kernel(req, ret_ref, rm, ra, cm, ca, rn, ran, cn, can, grads, done, out_sems):
    nodes, lists = ret_ref.shape[:2]
    tables = ((rm, ra, rn, ran), (cm, ca, cn, can))
    stores = []
    grads[...] = jnp.zeros_like(grads)
    for side, refs in enumerate(tables):
        for k in range(side, lists, 2):

            def one(node, carry, k=k, side=side):
                grads[side, req[node, side, k // 2]] += ret_ref[node, k].astype(F32)
                return carry

            lax.fori_loop(0, nodes, one, 0, unroll=4)
        at = 2 * side
        grad = grads[side]
        accum_new = refs[1][...] + grad * grad
        done[at + 1] = accum_new
        done[at] = refs[0][...] - LEARN_RATE * grad * lax.rsqrt(accum_new)
        for i in range(2):
            copy = pltpu.make_async_copy(done.at[at + i], refs[2 + i], out_sems.at[at + i])
            copy.start()
            stores.append(copy)
    for copy in stores:
        copy.wait()


def update(req, ret, row_master, row_accum, col_master, col_accum):
    shape = jax.ShapeDtypeStruct(row_master.shape, F32)
    return pl.pallas_call(
        update_kernel,
        out_shape=(shape,) * 4,
        grid_spec=pltpu.PrefetchScalarGridSpec(
            num_scalar_prefetch=1,
            grid=(),
            in_specs=[vmem_spec()] * 5,
            out_specs=(hbm_spec(),) * 4,
            scratch_shapes=[
                pltpu.VMEM((2,) + row_master.shape, F32),
                pltpu.VMEM((4,) + row_master.shape, F32),
                pltpu.SemaphoreType.DMA((4,)),
            ],
        ),
        compiler_params=pltpu.CompilerParams(vmem_limit_bytes=VMEM_LIMIT // 4),
        cost_estimate=pl.CostEstimate(
            flops=8 * row_master.size + ret.size,
            bytes_accessed=ret.size * 2 + 32 * row_master.size,
            transcendentals=2 * row_master.size,
        ),
        name="update",
    )(req, ret, row_master, row_accum, col_master, col_accum)


def exchange(x):
    return lax.all_to_all(x, AXES, split_axis=0, concat_axis=0, tiled=True)


def body(
    row_master, row_accum, col_master, col_accum, pairs, live, counts, row_marginal, col_marginal
):
    slots = pairs.shape[0]
    nodes = lax.axis_size(AXES)
    req = exchange(jnp.broadcast_to(pairs.T[None], (nodes, 2, slots)))
    row_low = row_master.astype(BF16)
    col_low = col_master.astype(BF16)
    got = exchange(pick(req, pairs, live, row_low, col_low, 0, slots))
    back = exchange(items(pairs, live, got, counts, row_marginal, col_marginal))
    return update(req, back, row_master, row_accum, col_master, col_accum)


def solution(mesh):
    table = P(None, AXES, None)
    return jax.shard_map(
        body,
        mesh=mesh,
        in_specs=(
            table,
            table,
            table,
            table,
            P(AXES, None),
            P(AXES),
            P(AXES, None, None),
            P(),
            P(),
        ),
        out_specs=(table,) * 4,
        check_vma=False,
    )
```
